256 devices in a mesh: ctx: 32 (over z, x), kvh: 8 (over y, core).
Axes of the slice: x: 4, y: 4, z: 8, core: 2. Of those that a mesh axis runs over, the one named last changes fastest.
Arguments:
- queries: bfloat16 [8192, 8192], P('ctx', 'kvh'), may hold values from -90 to 90
- keys: bfloat16 [8192, 1024], P('ctx', 'kvh'), may hold values from -4 to 4
- values: bfloat16 [8192, 1024], P('ctx', 'kvh'), may hold values from -6 to 6
- doc_lengths: int32 [16], replicated, may hold values from 1 to 2048, 8192 in all
Outputs:
- attended: bfloat16 [8192, 8192], P(('ctx', 'kvh'))
The draws below stay inside these ranges and needn't reach their ends.
Inputs may be any that keep to these rules, and one draw needn't show every extreme that they name: `doc_lengths`: the lengths sum to 8192; exactly one document, or more, has length 2048.
All inputs are finite; a program needn't handle non-finite values.
Results may differ from the reference program's by a relative error of at most 0.0036.
Values may be sent and summed in bfloat16 or wider, within the bound.
No kernel may reach another device: no remote copies, remote signals or barrier semaphores. Data moves between devices by JAX's collectives and lax.ppermute only.
A program may use at most 64 MiB of HBM per device.

```python
import math
import jax
import jax.numpy as jnp
import numpy as np
from jax import lax

KEY_VALUE_HEADS = 8
QUERY_PER_KEY = 8
HEAD_SIZE = 128
TOK_DEV = 256
PACKED_TOKENS = 8192
LONGEST_DOCUMENT = 2048
NDOCS = 16
N_CTX = 32


def shared_keys(key):
    inner_loop = jax.random.fold_in(key, 11)
    start_offset = jnp.clip(jax.random.normal(inner_loop, (PACKED_TOKENS, KEY_VALUE_HEADS * HEAD_SIZE), jnp.float32), -4.0, 4.0)
    rows = jnp.arange(PACKED_TOKENS, dtype=jnp.int32)[:, None]
    marked = rows % 61 == 3
    return jnp.where(marked, 0.997 * jnp.roll(start_offset, -1, axis=0), start_offset)


def draw_keys(key, part):
    return shared_keys(key).astype(jnp.bfloat16)


def draw_queries(key, part):
    key = jax.random.fold_in(key, 2)
    attention_output = jnp.clip(jax.random.normal(key, (PACKED_TOKENS, KEY_VALUE_HEADS * QUERY_PER_KEY * HEAD_SIZE), jnp.float32), -4.0, 4.0)
    return attention_output.astype(jnp.bfloat16)


def level_of(stream_key, dims, cuts, least, high):
    gain = 1.0
    for axis_at, blocks in cuts:
        draws = jax.random.uniform(jax.random.fold_in(jax.random.fold_in(stream_key, 6), axis_at), (blocks,), jnp.float32, least / len(cuts), high / len(cuts))
        gain = gain * jnp.repeat(jnp.exp(draws), dims[axis_at] // blocks).reshape((-1,) + (1,) * (len(dims) - 1 - axis_at))
    return gain


def length_profile(amount, total, bound, skew):
    weights = [(1 << 20) // math.isqrt(grade ** skew) + 1 for grade in range(2, amount + 1)]
    rest, holding = total - bound - (amount - 1), [1] * (amount - 1)
    while rest > 0:
        movable = [i for i in range(amount - 1) if holding[i] < bound]
        pool, budget = sum([weights[i] for i in movable]), rest
        for i in movable:
            addition = min(bound - holding[i], max(1, budget * weights[i] // pool), rest)
            holding[i] = holding[i] + addition
            rest = rest - addition
    return np.array([bound] + holding)


def ragged_sizes(stream_key, count, total, most, lean):
    if count == 2:
        one = jax.random.randint(stream_key, (), max(1, total - most), min(most, total - 1) + 1)
        return jnp.stack([one, total - one])
    lengths = jnp.asarray(length_profile(count, total, most, lean), jnp.int32)
    pairs = (count - 1) // 2
    donor, taker = lengths[1:1 + 2 * pairs:2], lengths[2:2 + 2 * pairs:2]
    room = jnp.minimum(donor - 1, most - taker)
    moved = jax.random.randint(jax.random.fold_in(stream_key, 1), (pairs,), 0, 1 << 20) % (room + 1)
    lengths = lengths.at[1:1 + 2 * pairs:2].set(donor - moved).at[2:2 + 2 * pairs:2].set(taker + moved)
    return lengths[jax.random.permutation(jax.random.fold_in(stream_key, 2), count)]


def noise(own_key, shape, scale, bound, cuts=(), held_as=jnp.bfloat16):
    entries = jax.random.normal(own_key, shape, jnp.float32) * scale
    if len(cuts) > 0:
        entries = level_of(own_key, shape, cuts, -0.22, 0.18) * entries
    return jnp.clip(entries, min=-bound, max=bound).astype(held_as)


def setup_inputs(seed: int = 0) -> dict:
    seeds = jax.random.split(jax.random.key(seed), 5)
    queries = draw_queries(jax.random.fold_in(seeds[4], 71), 0)
    keys = draw_keys(jax.random.fold_in(seeds[4], 71), 0)
    values = noise(seeds[2], (PACKED_TOKENS, KEY_VALUE_HEADS * HEAD_SIZE), 1.0, 6.0, ((0, 32), (1, 8)))
    doc_lengths = ragged_sizes(seeds[3], NDOCS, PACKED_TOKENS, LONGEST_DOCUMENT, 1).astype(jnp.int32)
    return dict(queries=queries, keys=keys, values=values, doc_lengths=doc_lengths)


def doc_of(positions, starts):
    return jnp.sum((starts[None, :] <= positions[:, None]).astype(jnp.int32), axis=1) - 1


def reference(queries, keys, values, doc_lengths):
    scale = 1.0 / (HEAD_SIZE ** 0.5)
    starts = (jnp.cumsum(doc_lengths) - doc_lengths).astype(jnp.int32)
    query_head_rows = queries.reshape(PACKED_TOKENS, KEY_VALUE_HEADS, QUERY_PER_KEY, HEAD_SIZE)
    key_padded_rows = jnp.concatenate([jnp.zeros((LONGEST_DOCUMENT, KEY_VALUE_HEADS * HEAD_SIZE), keys.dtype), keys], axis=0).reshape(PACKED_TOKENS + LONGEST_DOCUMENT, KEY_VALUE_HEADS, HEAD_SIZE)
    value_padded_rows = jnp.concatenate([jnp.zeros((LONGEST_DOCUMENT, KEY_VALUE_HEADS * HEAD_SIZE), values.dtype), values], axis=0).reshape(PACKED_TOKENS + LONGEST_DOCUMENT, KEY_VALUE_HEADS, HEAD_SIZE)
    window = LONGEST_DOCUMENT + TOK_DEV

    def one_block(block):
        first = (block * TOK_DEV).astype(jnp.int32)
        query_block = lax.dynamic_slice_in_dim(query_head_rows, first, TOK_DEV, 0)
        key_block = lax.dynamic_slice_in_dim(key_padded_rows, first, window, 0)
        value_block = lax.dynamic_slice_in_dim(value_padded_rows, first, window, 0)
        query_pos = first + jnp.arange(TOK_DEV, dtype=jnp.int32)
        key_pos = first - LONGEST_DOCUMENT + jnp.arange(window, dtype=jnp.int32)
        allowed = (doc_of(key_pos, starts)[None, :] == doc_of(query_pos, starts)[:, None]) & (key_pos[None, :] <= query_pos[:, None])

        def single_group(index):
            qg = lax.dynamic_index_in_dim(query_block, index, 1, False).astype(jnp.float32)
            kg = lax.dynamic_index_in_dim(key_block, index, 1, False).astype(jnp.float32)
            vg = lax.dynamic_index_in_dim(value_block, index, 1, False).astype(jnp.float32)
            score = jnp.einsum("tid,ud->itu", qg, kg) * scale
            score = jnp.where(allowed[None], score, jnp.float32(-1e30))
            top = jnp.max(score, axis=2, keepdims=True)
            weight = jnp.where(allowed[None], jnp.exp(score - top), jnp.float32(0.0))
            total = jnp.sum(weight, axis=2, keepdims=True)
            prob = weight.astype(jnp.bfloat16).astype(jnp.float32)
            mixed = jnp.einsum("itu,ud->itd", prob, vg) / total
            return jnp.transpose(mixed, (1, 0, 2)).astype(jnp.bfloat16)

        grouped_heads = lax.map(single_group, jnp.arange(KEY_VALUE_HEADS, dtype=jnp.int32))
        return jnp.transpose(grouped_heads, (1, 0, 2, 3))

    block_list = lax.map(one_block, jnp.arange(N_CTX, dtype=jnp.int32))
    return block_list.reshape(PACKED_TOKENS, KEY_VALUE_HEADS * QUERY_PER_KEY * HEAD_SIZE)
```

```python
import functools

import jax
import jax.numpy as jnp
from jax import lax
from jax.experimental import pallas as pl
from jax.experimental.pallas import tpu as pltpu
from jax.sharding import PartitionSpec as P

HEADS = 8
DIM = 128
ROWS = 256
NDOCS = 16
NX = 4
BIG = float(2**18)
SCALE = 1.0 / DIM**0.5
F32 = jnp.float32
BF16 = jnp.bfloat16


def bounds(len_ref):
    lane = lax.broadcasted_iota(jnp.int32, (1, DIM), 1)
    first = jnp.full((1, DIM), 2**30, jnp.int32)
    last = jnp.full((1, DIM), 2**30, jnp.int32)
    first = jnp.where(lane == NDOCS, -(2**30), first)
    last = jnp.where(lane == NDOCS, 0, last)
    at = jnp.int32(0)
    for d in range(NDOCS):
        first = jnp.where(lane == d, at, first)
        at = at + len_ref[d]
        last = jnp.where(lane == d, at, last)
    return first, last


def member(first, last, start):
    pos = start + lax.broadcasted_iota(jnp.int32, (ROWS, DIM), 0)
    return (pos >= first) & (pos < last)


def attend(kinds, has_state, final, *refs):
    n = len(kinds)
    len_ref, place_ref, q_ref = refs[:3]
    kv = refs[3 : 3 + n]
    rest = refs[3 + n :]
    if has_state:
        acc_in, tot_in, top_in = rest[:3]
        rest = rest[3:]
    if final:
        out_ref, qa_ref, ka_ref, va_ref = rest
    else:
        acc_out, tot_out, top_out, qa_ref, ka_ref, va_ref = rest
    place = place_ref[0]
    x = lax.rem(place, NX)
    row = place - x
    first, last = bounds(len_ref)
    qa_ref[...] = jnp.where(member(first, last, place * ROWS), 0.0, -BIG).astype(BF16)
    for b, (kind, d) in enumerate(kinds):
        if kind == "own":
            block = place
        elif kind == "z":
            block = place - NX * d
        elif kind == "row":
            block = row - NX + (x ^ d)
        else:
            other = x ^ d
            block = jnp.where(other < x, row, row - 2 * NX) + other
        rows = slice(b * ROWS, (b + 1) * ROWS)
        ka_ref[rows, :DIM] = kv[b][0]
        ka_ref[rows, DIM:] = jnp.where(member(first, last, block * ROWS), 1.0, 0.0).astype(BF16)
        va_ref[rows, :DIM] = kv[b][1]
        va_ref[rows, DIM:] = jnp.ones((ROWS, DIM), BF16)
    for h in range(HEADS):
        qq = jnp.concatenate([q_ref[:, h * DIM : (h + 1) * DIM], qa_ref[...]], axis=1)
        s = lax.dot_general(qq, ka_ref[...], (((1,), (1,)), ((), ())), preferred_element_type=F32)
        parts = []
        for b, (kind, _) in enumerate(kinds):
            c = s[:, b * ROWS : (b + 1) * ROWS]
            if kind == "own":
                r_id = lax.broadcasted_iota(jnp.int32, (ROWS, ROWS), 0)
                c_id = lax.broadcasted_iota(jnp.int32, (ROWS, ROWS), 1)
                c = jnp.where(c_id <= r_id, c, -BIG)
            parts += [c[:, :DIM], c[:, DIM:]]
        top = parts[0]
        for c in parts[1:]:
            top = jnp.maximum(top, c)
        top = jnp.broadcast_to(jnp.max(top, axis=1, keepdims=True), (ROWS, DIM))
        if has_state:
            old = top_in[h]
            top = jnp.maximum(old, top)
            keep = jnp.exp((old - top) * SCALE)
        p = jnp.concatenate([jnp.exp((c - top) * SCALE).astype(BF16) for c in parts], axis=1)
        mixed = jnp.dot(p, va_ref[...], preferred_element_type=F32)
        acc, tot = mixed[:, :DIM], mixed[:, DIM:]
        if has_state:
            acc = acc + acc_in[h] * keep
            tot = tot + tot_in[h] * keep
        if final:
            out_ref[:, h * DIM : (h + 1) * DIM] = (acc / tot).astype(BF16)
        else:
            acc_out[h] = acc
            tot_out[h] = tot
            top_out[h] = top


def attend_part(lengths, place, queries, parts, state=None, final=False):
    kinds = tuple(k for k, _ in parts)
    n = len(kinds)
    vmem = pl.BlockSpec(memory_space=pltpu.VMEM)
    smem = pl.BlockSpec(memory_space=pltpu.SMEM)
    arrays = [queries] + [a for _, a in parts] + list(state or ())
    part = jax.ShapeDtypeStruct((HEADS, ROWS, DIM), F32)
    out = jax.ShapeDtypeStruct((ROWS, HEADS * DIM), BF16)
    return pl.pallas_call(
        functools.partial(attend, kinds, state is not None, final),
        out_shape=out if final else (part,) * 3,
        in_specs=[smem, smem] + [vmem] * len(arrays),
        out_specs=vmem if final else (vmem,) * 3,
        scratch_shapes=[
            pltpu.VMEM((ROWS, DIM), BF16),
            pltpu.VMEM((n * ROWS, 2 * DIM), BF16),
            pltpu.VMEM((n * ROWS, 2 * DIM), BF16),
        ],
        cost_estimate=pl.CostEstimate(
            flops=8 * HEADS * ROWS * ROWS * DIM * n,
            bytes_accessed=1 << 20,
            transcendentals=HEADS * ROWS * ROWS * n,
        ),
        compiler_params=pltpu.CompilerParams(vmem_limit_bytes=40 * 2**20),
        name="attend",
    )(lengths, place, *arrays)


def per_device(queries, keys, values, doc_lengths):
    size = lax.axis_size("ctx")
    down = [(i, (i + NX) % size) for i in range(size)]
    flips = {d: [(i, i ^ d) for i in range(size)] for d in (1, 2, 3)}
    place = lax.axis_index("ctx")
    x = place % NX
    where = place.astype(jnp.int32).reshape(1)
    own = jnp.stack([keys, values])
    one = lax.ppermute(own, "ctx", down)
    row = {d: lax.ppermute(one, "ctx", flips[d]) for d in (2, 1, 3)}
    two = lax.ppermute(one, "ctx", down)
    mix = {}
    for d in (2, 1, 3):
        mix[d] = lax.ppermute(jnp.where(x < (x ^ d), own, two), "ctx", flips[d])
    parts = (
        [(("own", 0), own), (("z", 1), one), (("z", 2), two)]
        + [(("row", d), row[d]) for d in (1, 3, 2)]
        + [(("mix", d), mix[d]) for d in (1, 3, 2)]
    )
    attended = attend_part(doc_lengths, where, queries, parts, None, True)
    return lax.all_to_all(attended, "kvh", split_axis=0, concat_axis=1, tiled=True)


def solution(mesh):
    in_specs = (P("ctx", "kvh"), P("ctx", "kvh"), P("ctx", "kvh"), P())
    out_specs = P(("ctx", "kvh"), None)
    return jax.shard_map(
        per_device, mesh=mesh, in_specs=in_specs, out_specs=out_specs, check_vma=False
    )
```

```python
import functools

import jax
import jax.numpy as jnp
from jax import lax
from jax.experimental import pallas as pl
from jax.experimental.pallas import tpu as pltpu
from jax.sharding import PartitionSpec as P

HEADS = 8
DIM = 128
ROWS = 256
NDOCS = 16
NX = 4
NY = 4
SHARE = 32
BIG = float(2**18)
SCALE = 1.0 / DIM**0.5
F32 = jnp.float32
BF16 = jnp.bfloat16
VMEM = pl.BlockSpec(memory_space=pltpu.VMEM)
SMEM = pl.BlockSpec(memory_space=pltpu.SMEM)


def bounds(len_ref):
    lane = lax.broadcasted_iota(jnp.int32, (1, DIM), 1)
    first = jnp.full((1, DIM), 2**30, jnp.int32)
    last = jnp.full((1, DIM), 2**30, jnp.int32)
    first = jnp.where(lane == NDOCS, -(2**30), first)
    last = jnp.where(lane == NDOCS, 0, last)
    at = jnp.int32(0)
    for d in range(NDOCS):
        first = jnp.where(lane == d, at, first)
        at = at + len_ref[d]
        last = jnp.where(lane == d, at, last)
    return first, last


def own_row(r, y, core):
    return ((r & ~63) ^ (y << 6)) | ((r & 32) ^ (core << 5)) | (r & 31)


def block_of(kind, d, place, x):
    row = place - x
    if kind == "z":
        return place - NX * d
    if kind == "row":
        return row - NX + (x ^ d)
    other = x ^ d
    return jnp.where(other < x, row, row - 2 * NX) + other


def attend(kinds, lo, hi, opening, final, *refs):
    n = len(kinds)
    len_ref, place_ref = refs[:2]
    rest = list(refs[2:])
    place, y, core = place_ref[0], place_ref[1], place_ref[2]
    x = lax.rem(place, NX)
    q_ref = rest.pop(0)
    if not opening:
        qa_ref = rest.pop(0)
    kv = []
    while len(kv) < n:
        ref = rest.pop(0)
        if kinds[len(kv)] == ("either", 2):
            kv.append((ref, rest.pop(0)))
        elif len(ref.shape) == 4:
            kv += [ref.at[0], ref.at[1]]
        else:
            kv.append(ref)
    if not opening:
        state_in = rest[:3]
        rest = rest[3:]
    outs = rest[:-2]
    ka_ref, va_ref = rest[-2:]
    if not final:
        acc_out, tot_out, top_out = outs[:3]
        if opening:
            qp_ref, qa_ref = outs[3:]
    first, last = bounds(len_ref)
    if opening:
        for m in range(ROWS // SHARE):
            start = pl.multiple_of(own_row(m * SHARE, y, core), SHARE)
            qp_ref[m * SHARE : (m + 1) * SHARE, :] = q_ref[pl.ds(start, SHARE), :]
        pos = place * ROWS + own_row(lax.broadcasted_iota(jnp.int32, (ROWS, DIM), 0), y, core)
        qa_ref[...] = jnp.where((pos >= first) & (pos < last), 0.0, -BIG).astype(BF16)
        q_ref = qp_ref
    for b, (kind, d) in enumerate(kinds):
        rows = slice(b * ROWS, (b + 1) * ROWS)
        if kind == "either":
            late = x < (x ^ d)
            key = jnp.where(late, kv[b][1][0], kv[b][0][0])
            val = jnp.where(late, kv[b][1][1], kv[b][0][1])
        else:
            key, val = kv[b][0], kv[b][1]
        pos = block_of(kind, d, place, x) * ROWS + lax.broadcasted_iota(jnp.int32, (ROWS, DIM), 0)
        ka_ref[rows, :DIM] = key
        ka_ref[rows, DIM:] = jnp.where((pos >= first) & (pos < last), 1.0, 0.0).astype(BF16)
        va_ref[rows, :DIM] = val
        va_ref[rows, DIM:] = jnp.ones((ROWS, DIM), BF16)
    many = hi - lo
    for h in range(HEADS):
        cols = slice(h * DIM, (h + 1) * DIM)
        qq = jnp.concatenate([q_ref[lo:hi, cols], qa_ref[lo:hi, :]], axis=1)
        s = lax.dot_general(qq, ka_ref[...], (((1,), (1,)), ((), ())), preferred_element_type=F32)
        parts = []
        for b, (kind, d) in enumerate(kinds):
            c = s[:, b * ROWS : (b + 1) * ROWS]
            if (kind, d) == ("z", 0):
                r_id = own_row(lax.broadcasted_iota(jnp.int32, (many, ROWS), 0) + lo, y, core)
                c_id = lax.broadcasted_iota(jnp.int32, (many, ROWS), 1)
                c = jnp.where(c_id <= r_id, c, -BIG)
            parts += [c[:, :DIM], c[:, DIM:]]
        top = parts[0]
        for c in parts[1:]:
            top = jnp.maximum(top, c)
        top = jnp.broadcast_to(jnp.max(top, axis=1, keepdims=True), (many, DIM))
        if not opening:
            old = state_in[2][h, lo:hi, :]
            top = jnp.maximum(old, top)
            keep = jnp.exp((old - top) * SCALE)
        p = jnp.concatenate([jnp.exp((c - top) * SCALE).astype(BF16) for c in parts], axis=1)
        mixed = jnp.dot(p, va_ref[...], preferred_element_type=F32)
        acc, tot = mixed[:, :DIM], mixed[:, DIM:]
        if not opening:
            acc = acc + state_in[0][h, lo:hi, :] * keep
            tot = tot + state_in[1][h, lo:hi, :] * keep
        if final:
            res = (acc / tot).astype(BF16)
            for i, out in enumerate(outs):
                out[:, cols] = res[i * 2 * SHARE : (i + 1) * 2 * SHARE, :]
        else:
            acc_out[h] = acc
            tot_out[h] = tot
            top_out[h] = top


def attend_part(lengths, place, q, parts, state=None, final=False, lo=0, hi=ROWS):
    kinds = tuple(k for ks, _ in parts for k in ks)
    n = len(kinds)
    opening = state is None
    arrays = list(q)
    for _, a in parts:
        arrays += list(a) if isinstance(a, tuple) else [a]
    arrays += list(state or ())
    part = jax.ShapeDtypeStruct((HEADS, ROWS, DIM), F32)
    if final:
        outs = [jax.ShapeDtypeStruct((2 * SHARE, HEADS * DIM), BF16)] * ((hi - lo) // (2 * SHARE))
    else:
        outs = [part] * 3
        if opening:
            outs += [jax.ShapeDtypeStruct((ROWS, HEADS * DIM), BF16), jax.ShapeDtypeStruct((ROWS, DIM), BF16)]
    return pl.pallas_call(
        functools.partial(attend, kinds, lo, hi, opening, final),
        out_shape=outs,
        in_specs=[SMEM, SMEM] + [VMEM] * len(arrays),
        out_specs=[VMEM] * len(outs),
        scratch_shapes=[pltpu.VMEM((n * ROWS, 2 * DIM), BF16)] * 2,
        cost_estimate=pl.CostEstimate(
            flops=8 * HEADS * (hi - lo) * ROWS * DIM * n,
            bytes_accessed=1 << 20,
            transcendentals=HEADS * (hi - lo) * ROWS * n,
        ),
        compiler_params=pltpu.CompilerParams(vmem_limit_bytes=40 * 2**20),
        name="attend",
    )(lengths, place, *arrays)


def lay_out(place_ref, *refs):
    y, core = place_ref[1], place_ref[2]
    pieces, got, out, sems = refs[:NY], refs[NY], refs[NY + 1], refs[NY + 2]
    width = HEADS * DIM
    copies = []
    for d in range(NY):
        for k in range(2):
            src = got.at[d] if k else pieces[d].at[pl.ds(0, SHARE), :]
            at = pl.multiple_of((((y ^ d) << 1) + (core ^ k)) * width, width)
            copies.append(pltpu.make_async_copy(src, out.at[:, pl.ds(at, width)], sems.at[2 * d + k]))
    for c in copies:
        c.start()
    for c in copies:
        c.wait()


def exchange(place, pieces):
    size = lax.axis_size("kvh")
    flip = lambda m: [(i, i ^ m) for i in range(size)]
    held = {0: pieces[0]}
    for d in (2, 1, 3):
        held[d] = lax.ppermute(pieces[d], "kvh", flip(2 * d))
    held = [held[d] for d in range(NY)]
    got = lax.ppermute(jnp.stack([h[SHARE:] for h in held]), "kvh", flip(1))
    anywhere = pl.BlockSpec(memory_space=pl.ANY)
    return pl.pallas_call(
        lay_out,
        out_shape=jax.ShapeDtypeStruct((SHARE, size * HEADS * DIM), BF16),
        in_specs=[SMEM] + [VMEM] * (NY + 1),
        out_specs=anywhere,
        scratch_shapes=[pltpu.SemaphoreType.DMA((2 * NY,))],
        compiler_params=pltpu.CompilerParams(vmem_limit_bytes=40 * 2**20),
        name="lay_out",
    )(place, *held, got)


def per_device(queries, keys, values, doc_lengths):
    size = lax.axis_size("ctx")
    down = [(i, (i + NX) % size) for i in range(size)]
    flip = lambda d: [(i, i ^ d) for i in range(size)]
    place = lax.axis_index("ctx")
    kvh = lax.axis_index("kvh")
    x = place % NX
    where = jnp.stack([place, kvh // 2, kvh % 2]).astype(jnp.int32)
    send = functools.partial(lax.ppermute, axis_name="ctx")
    own = jnp.stack([keys, values])
    one = send(own, perm=down)
    across = send(own, perm=flip(2))
    two = send(one, perm=down)
    one_across = send(across, perm=down)
    low = jnp.stack([one, jnp.where(x & 1 == 0, own, two)])
    high = jnp.stack([one, jnp.where(x & 2 == 0, own, two)])
    near = send(low, perm=flip(1))
    far = send(high, perm=flip(3))
    two_across = send(one_across, perm=down)
    p_own = ((("z", 0),), own)
    p_one = ((("z", 1),), one)
    p_two = ((("z", 2),), two)
    p_across = ((("row", 2),), one_across)
    p_near = ((("row", 1), ("mix", 1)), near)
    p_far = ((("row", 3), ("mix", 3)), far)
    p_either = ((("either", 2),), (across, two_across))
    groups = [[p_own, p_one], [p_two, p_across], [p_near, p_far, p_either]]
    *state, qp, qa = attend_part(doc_lengths, where, (queries,), groups[0])
    for g in groups[1:-1]:
        state = attend_part(doc_lengths, where, (qp, qa), g, state)
    pieces = attend_part(doc_lengths, where, (qp, qa), groups[-1], state, True)
    return exchange(where, pieces)


def solution(mesh):
    in_specs = (P("ctx", "kvh"), P("ctx", "kvh"), P("ctx", "kvh"), P())
    out_specs = P(("ctx", "kvh"), None)
    return jax.shard_map(
        per_device, mesh=mesh, in_specs=in_specs, out_specs=out_specs, check_vma=False
    )
```

```python
import functools
import math

import jax
import jax.numpy as jnp
from jax import lax
from jax.experimental import pallas as pl
from jax.experimental.pallas import tpu as pltpu
from jax.sharding import PartitionSpec as P

HEADS = 8
DIM = 128
ROWS = 256
NDOCS = 16
NX = 4
NY = 4
SHARE = 32
BIG = float(2**18)
SCALE = math.log2(math.e) / DIM**0.5
F32 = jnp.float32
BF16 = jnp.bfloat16
VMEM = pl.BlockSpec(memory_space=pltpu.VMEM)
SMEM = pl.BlockSpec(memory_space=pltpu.SMEM)


def bounds(len_ref):
    lane = lax.broadcasted_iota(jnp.int32, (1, DIM), 1)
    first = jnp.full((1, DIM), 2**30, jnp.int32)
    last = jnp.full((1, DIM), 2**30, jnp.int32)
    first = jnp.where(lane == NDOCS, -(2**30), first)
    last = jnp.where(lane == NDOCS, 0, last)
    at = jnp.int32(0)
    for d in range(NDOCS):
        first = jnp.where(lane == d, at, first)
        at = at + len_ref[d]
        last = jnp.where(lane == d, at, last)
    return first, last


def reach(len_ref, place):
    at = jnp.int32(0)
    begin = jnp.int32(0)
    for d in range(NDOCS):
        begin = jnp.where(at <= place * ROWS, at, begin)
        at = at + len_ref[d]
    return begin


def own_row(r, y, core):
    return ((r & ~63) ^ (y << 6)) | ((r & 32) ^ (core << 5)) | (r & 31)


def block_of(kind, d, place, x):
    row = place - x
    if kind == "z":
        return place - NX * d
    if kind == "row":
        return row - NX + (x ^ d)
    other = x ^ d
    return jnp.where(other < x, row, row - 2 * NX) + other


def attend(kinds, opening, final, *refs):
    n = len(kinds)
    len_ref, place_ref = refs[:2]
    rest = list(refs[2:])
    place, y, core = place_ref[0], place_ref[1], place_ref[2]
    x = lax.rem(place, NX)
    q_ref = rest.pop(0)
    if not opening:
        qa_ref = rest.pop(0)
    kv = []
    while len(kv) < n:
        ref = rest.pop(0)
        if kinds[len(kv)] == ("either", 2):
            kv.append((ref, rest.pop(0)))
        elif len(ref.shape) == 4:
            kv += [ref.at[0], ref.at[1]]
        else:
            kv.append(ref)
    if not opening:
        state_in = rest[:3]
        rest = rest[3:]
    outs = rest[:-2]
    ka_ref, va_ref = rest[-2:]
    if not final:
        acc_out, tot_out, top_out = outs[:3]
        if opening:
            qp_ref, qa_ref = outs[3:]
    first, last = bounds(len_ref)
    if opening:
        for m in range(ROWS // SHARE):
            start = pl.multiple_of(own_row(m * SHARE, y, core), SHARE)
            qp_ref[m * SHARE : (m + 1) * SHARE, :] = q_ref[pl.ds(start, SHARE), :]
        pos = place * ROWS + own_row(lax.broadcasted_iota(jnp.int32, (ROWS, DIM), 0), y, core)
        qa_ref[...] = jnp.where((pos >= first) & (pos < last), 0.0, -BIG).astype(BF16)
        q_ref = qp_ref
    front, back = jnp.int32(0), jnp.int32(n - 1)
    begin = reach(len_ref, place)
    for b, (kind, d) in enumerate(kinds):
        if kind == "either":
            late = x < (x ^ d)
            key = jnp.where(late, kv[b][1][0], kv[b][0][0])
            val = jnp.where(late, kv[b][1][1], kv[b][0][1])
        else:
            key, val = kv[b][0], kv[b][1]
        start = block_of(kind, d, place, x) * ROWS
        rows = slice(b * ROWS, (b + 1) * ROWS)
        at = rows
        if final:
            used = (start + ROWS > begin).astype(jnp.int32)
            at = pl.ds(pl.multiple_of(jnp.where(used == 1, front, back) * ROWS, ROWS), ROWS)
            front, back = front + used, back - (1 - used)
        pos = start + lax.broadcasted_iota(jnp.int32, (ROWS, DIM), 0)
        ka_ref[:DIM, at] = key.T
        ka_ref[DIM:, at] = jnp.where((pos >= first) & (pos < last), 1.0, 0.0).astype(BF16).T
        va_ref[at, :DIM] = val
        va_ref[rows, DIM:] = jnp.ones((ROWS, DIM), BF16)

    def scores(h, m):
        qq = jnp.concatenate([q_ref[:, h * DIM : (h + 1) * DIM], qa_ref[...]], axis=1)
        return jnp.dot(qq, ka_ref[:, : m * ROWS], preferred_element_type=F32)

    def fold(m):
        ahead = scores(0, m) if m else None
        for h in range(HEADS):
            cols = slice(h * DIM, (h + 1) * DIM)
            if m:
                s = ahead
                if h + 1 < HEADS:
                    ahead = scores(h + 1, m)
                parts = []
                for b in range(m):
                    c = s[:, b * ROWS : (b + 1) * ROWS]
                    if kinds[b] == ("z", 0):
                        r_id = own_row(lax.broadcasted_iota(jnp.int32, (ROWS, ROWS), 0), y, core)
                        c_id = lax.broadcasted_iota(jnp.int32, (ROWS, ROWS), 1)
                        c = jnp.where(c_id <= r_id, c, -BIG)
                    parts += [c[:, :DIM], c[:, DIM:]]
                top = parts[0]
                for c in parts[1:]:
                    top = jnp.maximum(top, c)
                top = jnp.broadcast_to(jnp.max(top, axis=1, keepdims=True), (ROWS, DIM))
                if not opening:
                    old = state_in[2][h]
                    top = jnp.maximum(old, top)
                    keep = jnp.exp2((old - top) * SCALE)
                p = [jnp.exp2((c - top) * SCALE).astype(BF16) for c in parts]
                mixed = jnp.dot(
                    jnp.concatenate(p, axis=1), va_ref[: m * ROWS, :], preferred_element_type=F32
                )
                acc, tot = mixed[:, :DIM], mixed[:, DIM:]
                if not opening:
                    acc = acc + state_in[0][h] * keep
                    tot = tot + state_in[1][h] * keep
            else:
                acc, tot = state_in[0][h], state_in[1][h]
            if final:
                res = (acc / tot).astype(BF16)
                for i, out in enumerate(outs):
                    out[:, cols] = res[i * 2 * SHARE : (i + 1) * 2 * SHARE, :]
            else:
                acc_out[h] = acc
                tot_out[h] = tot
                top_out[h] = top

    if final:
        sizes = (0, 2, n)
        for i, m in enumerate(sizes):
            fits = front <= m
            if i:
                fits = fits & (front > sizes[i - 1])
            pl.when(fits)(functools.partial(fold, m))
    else:
        fold(n)


def attend_part(lengths, place, q, parts, state=None, final=False):
    kinds = tuple(k for ks, _ in parts for k in ks)
    n = len(kinds)
    opening = state is None
    arrays = list(q)
    for _, a in parts:
        arrays += list(a) if isinstance(a, tuple) else [a]
    arrays += list(state or ())
    part = jax.ShapeDtypeStruct((HEADS, ROWS, DIM), F32)
    if final:
        outs = [jax.ShapeDtypeStruct((2 * SHARE, HEADS * DIM), BF16)] * NY
    else:
        outs = [part] * 3
        if opening:
            outs += [jax.ShapeDtypeStruct((ROWS, HEADS * DIM), BF16), jax.ShapeDtypeStruct((ROWS, DIM), BF16)]
    return pl.pallas_call(
        functools.partial(attend, kinds, opening, final),
        out_shape=outs,
        in_specs=[SMEM, SMEM] + [VMEM] * len(arrays),
        out_specs=[VMEM] * len(outs),
        scratch_shapes=[pltpu.VMEM((2 * DIM, n * ROWS), BF16), pltpu.VMEM((n * ROWS, 2 * DIM), BF16)],
        cost_estimate=pl.CostEstimate(
            flops=8 * HEADS * ROWS * ROWS * DIM * n,
            bytes_accessed=1 << 20,
            transcendentals=HEADS * ROWS * ROWS * n,
        ),
        compiler_params=pltpu.CompilerParams(vmem_limit_bytes=40 * 2**20),
        name="attend",
    )(lengths, place, *arrays)


def lay_out(place_ref, *refs):
    y, core = place_ref[1], place_ref[2]
    pieces, got, out, sems = refs[:NY], refs[NY], refs[NY + 1], refs[NY + 2]
    width = HEADS * DIM
    copies = []
    for d in range(NY):
        for k in range(2):
            src = got.at[d] if k else pieces[d].at[pl.ds(0, SHARE), :]
            at = pl.multiple_of((((y ^ d) << 1) + (core ^ k)) * width, width)
            copies.append(pltpu.make_async_copy(src, out.at[:, pl.ds(at, width)], sems.at[2 * d + k]))
    for c in copies:
        c.start()
    for c in copies:
        c.wait()


def exchange(place, pieces):
    size = lax.axis_size("kvh")
    flip = lambda m: [(i, i ^ m) for i in range(size)]
    held = {0: pieces[0]}
    for d in (2, 1, 3):
        held[d] = lax.ppermute(pieces[d], "kvh", flip(2 * d))
    held = [held[d] for d in range(NY)]
    got = lax.ppermute(jnp.stack([h[SHARE:] for h in held]), "kvh", flip(1))
    anywhere = pl.BlockSpec(memory_space=pl.ANY)
    return pl.pallas_call(
        lay_out,
        out_shape=jax.ShapeDtypeStruct((SHARE, size * HEADS * DIM), BF16),
        in_specs=[SMEM] + [VMEM] * (NY + 1),
        out_specs=anywhere,
        scratch_shapes=[pltpu.SemaphoreType.DMA((2 * NY,))],
        compiler_params=pltpu.CompilerParams(vmem_limit_bytes=40 * 2**20),
        name="lay_out",
    )(place, *held, got)


def per_device(queries, keys, values, doc_lengths):
    size = lax.axis_size("ctx")
    down = [(i, (i + NX) % size) for i in range(size)]
    flip = lambda d: [(i, i ^ d) for i in range(size)]
    place = lax.axis_index("ctx")
    kvh = lax.axis_index("kvh")
    x = place % NX
    where = jnp.stack([place, kvh // 2, kvh % 2]).astype(jnp.int32)
    send = functools.partial(lax.ppermute, axis_name="ctx")
    own = jnp.stack([keys, values])
    one = send(own, perm=down)
    across = send(own, perm=flip(2))
    two = send(one, perm=down)
    p_own = ((("z", 0),), own)
    p_one = ((("z", 1),), one)
    *state, qp, qa = attend_part(doc_lengths, where, (queries,), [p_own])
    two, state = lax.optimization_barrier((two, state))
    one_across = send(across, perm=down)
    low = jnp.stack([one, jnp.where(x & 1 == 0, own, two)])
    high = jnp.stack([one, jnp.where(x & 2 == 0, own, two)])
    near = send(low, perm=flip(1))
    far = send(high, perm=flip(3))
    two_across = send(one_across, perm=down)
    p_two = ((("z", 2),), two)
    p_across = ((("row", 2),), one_across)
    p_near = ((("row", 1), ("mix", 1)), near)
    p_far = ((("row", 3), ("mix", 3)), far)
    p_either = ((("either", 2),), (across, two_across))
    state = attend_part(doc_lengths, where, (qp, qa), [p_one, p_two, p_across], state)
    last = [p_near, p_far, p_either]
    pieces = attend_part(doc_lengths, where, (qp, qa), last, state, True)
    return exchange(where, pieces)


def solution(mesh):
    in_specs = (P("ctx", "kvh"), P("ctx", "kvh"), P("ctx", "kvh"), P())
    out_specs = P(("ctx", "kvh"), None)
    return jax.shard_map(
        per_device, mesh=mesh, in_specs=in_specs, out_specs=out_specs, check_vma=False
    )
```

```python
import functools
import math

import jax
import jax.numpy as jnp
from jax import lax
from jax.experimental import pallas as pl
from jax.experimental.pallas import tpu as pltpu
from jax.sharding import PartitionSpec as P

HEADS = 8
DIM = 128
ROWS = 256
NDOCS = 16
NX = 4
NY = 4
SHARE = 32
BIG = float(2**18)
SCALE = math.log2(math.e) / DIM**0.5
F32 = jnp.float32
BF16 = jnp.bfloat16
VMEM = pl.BlockSpec(memory_space=pltpu.VMEM)
SMEM = pl.BlockSpec(memory_space=pltpu.SMEM)


def bounds(len_ref):
    lane = lax.broadcasted_iota(jnp.int32, (1, DIM), 1)
    first = jnp.full((1, DIM), 2**30, jnp.int32)
    last = jnp.full((1, DIM), 2**30, jnp.int32)
    first = jnp.where(lane == NDOCS, -(2**30), first)
    last = jnp.where(lane == NDOCS, 0, last)
    at = jnp.int32(0)
    for d in range(NDOCS):
        first = jnp.where(lane == d, at, first)
        at = at + len_ref[d]
        last = jnp.where(lane == d, at, last)
    return first, last


def position():
    kvh = lax.axis_index("kvh").astype(jnp.int32)
    return lax.axis_index("ctx").astype(jnp.int32), kvh // 2, kvh % 2


def reach(len_ref, place):
    at = jnp.int32(0)
    begin = jnp.int32(0)
    for d in range(NDOCS):
        begin = jnp.where(at <= place * ROWS, at, begin)
        at = at + len_ref[d]
    return begin


def own_row(r, y, core):
    return ((r & ~63) ^ (y << 6)) | ((r & 32) ^ (core << 5)) | (r & 31)


def block_of(kind, d, place, x):
    row = place - x
    if kind == "z":
        return place - NX * d
    if kind == "row":
        return row - NX + (x ^ d)
    other = x ^ d
    return jnp.where(other < x, row, row - 2 * NX) + other


def attend(kinds, opening, final, *refs):
    n = len(kinds)
    len_ref = refs[0]
    rest = list(refs[1:])
    place, y, core = position()
    x = lax.rem(place, NX)
    q_ref = rest.pop(0)
    if not opening:
        qa_ref = rest.pop(0)
    kv = []
    while len(kv) < n:
        ref = rest.pop(0)
        if kinds[len(kv)] == ("either", 2):
            kv.append((ref, rest.pop(0)))
        elif len(ref.shape) == 4:
            kv += [ref.at[0], ref.at[1]]
        else:
            kv.append(ref)
    if not opening:
        state_in = rest[:3]
        rest = rest[3:]
    outs = rest[:-2]
    ka_ref, va_ref = rest[-2:]
    if not final:
        acc_out, tot_out, top_out = outs[:3]
        if opening:
            qp_ref, qa_ref = outs[3:]
    first, last = bounds(len_ref)
    if opening:
        for m in range(ROWS // SHARE):
            start = pl.multiple_of(own_row(m * SHARE, y, core), SHARE)
            qp_ref[m * SHARE : (m + 1) * SHARE, :] = q_ref[pl.ds(start, SHARE), :]
        pos = place * ROWS + own_row(lax.broadcasted_iota(jnp.int32, (ROWS, DIM), 0), y, core)
        qa_ref[...] = jnp.where((pos >= first) & (pos < last), 0.0, -BIG).astype(BF16)
        q_ref = qp_ref
    front = jnp.int32(0)
    begin = reach(len_ref, place)
    va_ref[:, DIM:] = jnp.ones((n * ROWS, DIM), BF16)
    for b, (kind, d) in enumerate(kinds):
        start = block_of(kind, d, place, x) * ROWS

        def place_block(at, b=b, kind=kind, d=d, start=start):
            if kind == "either":
                late = x < (x ^ d)
                key = jnp.where(late, kv[b][1][0], kv[b][0][0])
                val = jnp.where(late, kv[b][1][1], kv[b][0][1])
            else:
                key, val = kv[b][0], kv[b][1]
            pos = start + lax.broadcasted_iota(jnp.int32, (ROWS, DIM), 0)
            ka_ref[:DIM, at] = key.T
            ka_ref[DIM:, at] = jnp.where((pos >= first) & (pos < last), 1.0, 0.0).astype(BF16).T
            va_ref[at, :DIM] = val

        if opening:
            place_block(slice(b * ROWS, (b + 1) * ROWS))
        else:
            used = start + ROWS > begin
            at = pl.ds(pl.multiple_of(front * ROWS, ROWS), ROWS)
            pl.when(used)(functools.partial(place_block, at))
            front = front + used.astype(jnp.int32)

    def scores(h, m):
        qq = jnp.concatenate([q_ref[:, h * DIM : (h + 1) * DIM], qa_ref[...]], axis=1)
        return jnp.dot(qq, ka_ref[:, : m * ROWS], preferred_element_type=F32)

    def fold(m):
        ahead = scores(0, m) if m else None
        for h in range(HEADS):
            cols = slice(h * DIM, (h + 1) * DIM)
            if m:
                s = ahead
                if h + 1 < HEADS:
                    ahead = scores(h + 1, m)
                parts = []
                for b in range(m):
                    c = s[:, b * ROWS : (b + 1) * ROWS]
                    if kinds[b] == ("z", 0):
                        r_id = own_row(lax.broadcasted_iota(jnp.int32, (ROWS, ROWS), 0), y, core)
                        c_id = lax.broadcasted_iota(jnp.int32, (ROWS, ROWS), 1)
                        c = jnp.where(c_id <= r_id, c, -BIG)
                    parts += [c[:, :DIM], c[:, DIM:]]
                top = parts[0]
                for c in parts[1:]:
                    top = jnp.maximum(top, c)
                top = jnp.broadcast_to(jnp.max(top, axis=1, keepdims=True), (ROWS, DIM))
                if not opening:
                    old = state_in[2][h]
                    top = jnp.maximum(old, top)
                    keep = jnp.exp2((old - top) * SCALE)
                p = [jnp.exp2((c - top) * SCALE).astype(BF16) for c in parts]
                mixed = jnp.dot(
                    jnp.concatenate(p, axis=1), va_ref[: m * ROWS, :], preferred_element_type=F32
                )
                acc, tot = mixed[:, :DIM], mixed[:, DIM:]
                if not opening:
                    acc = acc + state_in[0][h] * keep
                    tot = tot + state_in[1][h] * keep
            else:
                acc, tot, top = state_in[0][h], state_in[1][h], state_in[2][h]
            if final:
                res = (acc / tot).astype(BF16)
                for i, out in enumerate(outs):
                    out[:, cols] = res[i * 2 * SHARE : (i + 1) * 2 * SHARE, :]
            else:
                acc_out[h] = acc
                tot_out[h] = tot
                top_out[h] = top

    if opening:
        fold(n)
    else:
        for m in range(n + 1):
            pl.when(front == m)(functools.partial(fold, m))


def attend_part(lengths, q, parts, state=None, final=False):
    kinds = tuple(k for ks, _ in parts for k in ks)
    n = len(kinds)
    opening = state is None
    arrays = list(q)
    for _, a in parts:
        arrays += list(a) if isinstance(a, tuple) else [a]
    arrays += list(state or ())
    part = jax.ShapeDtypeStruct((HEADS, ROWS, DIM), F32)
    if final:
        outs = [jax.ShapeDtypeStruct((2 * SHARE, HEADS * DIM), BF16)] * NY
    else:
        outs = [part] * 3
        if opening:
            outs += [jax.ShapeDtypeStruct((ROWS, HEADS * DIM), BF16), jax.ShapeDtypeStruct((ROWS, DIM), BF16)]
    return pl.pallas_call(
        functools.partial(attend, kinds, opening, final),
        out_shape=outs,
        in_specs=[SMEM] + [VMEM] * len(arrays),
        out_specs=[VMEM] * len(outs),
        scratch_shapes=[pltpu.VMEM((2 * DIM, n * ROWS), BF16), pltpu.VMEM((n * ROWS, 2 * DIM), BF16)],
        cost_estimate=pl.CostEstimate(
            flops=8 * HEADS * ROWS * ROWS * DIM * n,
            bytes_accessed=1 << 20,
            transcendentals=HEADS * ROWS * ROWS * n,
        ),
        compiler_params=pltpu.CompilerParams(vmem_limit_bytes=16 * 2**20),
        name="attend",
    )(lengths, *arrays)


def lay_out(*refs):
    _, y, core = position()
    pieces, got, out, sems = refs[:NY], refs[NY], refs[NY + 1], refs[NY + 2]
    width = HEADS * DIM
    copies = []
    for d in range(NY):
        for k in range(2):
            src = got.at[d] if k else pieces[d].at[pl.ds(0, SHARE), :]
            at = pl.multiple_of((((y ^ d) << 1) + (core ^ k)) * width, width)
            copies.append(pltpu.make_async_copy(src, out.at[:, pl.ds(at, width)], sems.at[2 * d + k]))
    for c in copies:
        c.start()
    for c in copies:
        c.wait()


def exchange(pieces):
    size = lax.axis_size("kvh")
    flip = lambda m: [(i, i ^ m) for i in range(size)]
    held = {0: pieces[0]}
    for d in (2, 1, 3):
        held[d] = lax.ppermute(pieces[d], "kvh", flip(2 * d))
    held = [held[d] for d in range(NY)]
    got = lax.ppermute(jnp.stack([h[SHARE:] for h in held]), "kvh", flip(1))
    anywhere = pl.BlockSpec(memory_space=pl.ANY)
    return pl.pallas_call(
        lay_out,
        out_shape=jax.ShapeDtypeStruct((SHARE, size * HEADS * DIM), BF16),
        in_specs=[VMEM] * (NY + 1),
        out_specs=anywhere,
        scratch_shapes=[pltpu.SemaphoreType.DMA((2 * NY,))],
        compiler_params=pltpu.CompilerParams(vmem_limit_bytes=16 * 2**20),
        name="lay_out",
    )(*held, got)


def per_device(queries, keys, values, doc_lengths):
    size = lax.axis_size("ctx")
    down = [(i, (i + NX) % size) for i in range(size)]
    flip = lambda d: [(i, i ^ d) for i in range(size)]
    place = lax.axis_index("ctx")
    x = place % NX
    send = functools.partial(lax.ppermute, axis_name="ctx")
    own = jnp.stack([keys, values])
    one = send(own, perm=down)
    across = send(own, perm=flip(2))
    two = send(one, perm=down)
    p_one = ((("z", 1),), one)
    across, mine = lax.optimization_barrier((across, own))
    p_own = ((("z", 0),), mine)
    *state, qp, qa = attend_part(doc_lengths, (queries,), [p_own])
    two, state = lax.optimization_barrier((two, state))
    one_across = send(across, perm=down)
    low = jnp.stack([one, jnp.where(x & 1 == 0, own, two)])
    high = jnp.stack([one, jnp.where(x & 2 == 0, own, two)])
    near = send(low, perm=flip(1))
    far = send(high, perm=flip(3))
    two_across = send(one_across, perm=down)
    p_two = ((("z", 2),), two)
    p_across = ((("row", 2),), one_across)
    p_near = ((("row", 1), ("mix", 1)), near)
    p_far = ((("row", 3), ("mix", 3)), far)
    p_either = ((("either", 2),), (across, two_across))
    state = attend_part(doc_lengths, (qp, qa), [p_one, p_two, p_across], state)
    last = [p_near, p_far, p_either]
    pieces = attend_part(doc_lengths, (qp, qa), last, state, True)
    return exchange(pieces)


def solution(mesh):
    in_specs = (P("ctx", "kvh"), P("ctx", "kvh"), P("ctx", "kvh"), P())
    out_specs = P(("ctx", "kvh"), None)
    return jax.shard_map(
        per_device, mesh=mesh, in_specs=in_specs, out_specs=out_specs, check_vma=False
    )
```

```python
import functools
import math

import jax
import jax.numpy as jnp
from jax import lax
from jax.experimental import pallas as pl
from jax.experimental.pallas import tpu as pltpu
from jax.sharding import PartitionSpec as P

HEADS = 8
DIM = 128
ROWS = 256
NDOCS = 16
NX = 4
NY = 4
SHARE = 32
BIG = float(2**18)
SCALE = math.log2(math.e) / DIM**0.5
F32 = jnp.float32
BF16 = jnp.bfloat16
VMEM = pl.BlockSpec(memory_space=pltpu.VMEM)
SMEM = pl.BlockSpec(memory_space=pltpu.SMEM)


def bounds(len_ref):
    lane = lax.broadcasted_iota(jnp.int32, (1, DIM), 1)
    first = jnp.full((1, DIM), 2**30, jnp.int32)
    last = jnp.full((1, DIM), 2**30, jnp.int32)
    first = jnp.where(lane == NDOCS, -(2**30), first)
    last = jnp.where(lane == NDOCS, 0, last)
    at = jnp.int32(0)
    for d in range(NDOCS):
        first = jnp.where(lane == d, at, first)
        at = at + len_ref[d]
        last = jnp.where(lane == d, at, last)
    return first, last


def position():
    kvh = lax.axis_index("kvh").astype(jnp.int32)
    return lax.axis_index("ctx").astype(jnp.int32), kvh // 2, kvh % 2


def reach(len_ref, place):
    at = jnp.int32(0)
    begin = jnp.int32(0)
    for d in range(NDOCS):
        begin = jnp.where(at <= place * ROWS, at, begin)
        at = at + len_ref[d]
    return begin


def own_row(r, y, core):
    return ((r & ~63) ^ (y << 6)) | ((r & 32) ^ (core << 5)) | (r & 31)


def block_of(kind, d, place, x):
    row = place - x
    if kind == "z":
        return place - NX * d
    if kind == "row":
        return row - NX + (x ^ d)
    other = x ^ d
    return jnp.where(other < x, row, row - 2 * NX) + other


def attend(kinds, opening, final, *refs):
    n = len(kinds)
    len_ref = refs[0]
    rest = list(refs[1:])
    place, y, core = position()
    x = lax.rem(place, NX)
    q_ref = rest.pop(0)
    if not opening:
        qa_ref = rest.pop(0)
    kv = []
    while len(kv) < n:
        ref = rest.pop(0)
        if kinds[len(kv)] == ("either", 2):
            kv.append((ref, rest.pop(0)))
        elif len(ref.shape) == 4:
            kv += [ref.at[0], ref.at[1]]
        else:
            kv.append(ref)
    if not opening:
        state_in = rest[:3]
        rest = rest[3:]
    outs = rest[:-2]
    ka_ref, va_ref = rest[-2:]
    if not final:
        acc_out, tot_out, top_out = outs[:3]
        if opening:
            qp_ref, qa_ref = outs[3:]
    first, last = bounds(len_ref)
    if opening:
        for m in range(ROWS // SHARE):
            start = pl.multiple_of(own_row(m * SHARE, y, core), SHARE)
            qp_ref[m * SHARE : (m + 1) * SHARE, :] = q_ref[pl.ds(start, SHARE), :]
        pos = place * ROWS + own_row(lax.broadcasted_iota(jnp.int32, (ROWS, DIM), 0), y, core)
        qa_ref[...] = jnp.where((pos >= first) & (pos < last), 0.0, -BIG).astype(BF16)
        q_ref = qp_ref
    front = jnp.int32(0)
    begin = reach(len_ref, place)
    va_ref[:, DIM:] = jnp.ones((n * ROWS, DIM), BF16)
    for b, (kind, d) in enumerate(kinds):
        start = block_of(kind, d, place, x) * ROWS

        def place_block(at, b=b, kind=kind, d=d, start=start):
            if kind == "either":
                late = x < (x ^ d)
                key = jnp.where(late, kv[b][1][0], kv[b][0][0])
                val = jnp.where(late, kv[b][1][1], kv[b][0][1])
            else:
                key, val = kv[b][0], kv[b][1]
            pos = start + lax.broadcasted_iota(jnp.int32, (ROWS, DIM), 0)
            ka_ref[:DIM, at] = key.T
            ka_ref[DIM:, at] = jnp.where((pos >= first) & (pos < last), 1.0, 0.0).astype(BF16).T
            va_ref[at, :DIM] = val

        if opening:
            place_block(slice(b * ROWS, (b + 1) * ROWS))
        else:
            used = start + ROWS > begin
            at = pl.ds(pl.multiple_of(front * ROWS, ROWS), ROWS)
            pl.when(used)(functools.partial(place_block, at))
            front = front + used.astype(jnp.int32)

    def scores(h, m):
        qq = jnp.concatenate([q_ref[:, h * DIM : (h + 1) * DIM], qa_ref[...]], axis=1)
        return jnp.dot(qq, ka_ref[:, : m * ROWS], preferred_element_type=F32)

    def fold(m):
        ahead = scores(0, m) if m else None
        for h in range(HEADS):
            cols = slice(h * DIM, (h + 1) * DIM)
            if m:
                s = ahead
                if h + 1 < HEADS:
                    ahead = scores(h + 1, m)
                parts = []
                for b in range(m):
                    c = s[:, b * ROWS : (b + 1) * ROWS]
                    if kinds[b] == ("z", 0):
                        r_id = own_row(lax.broadcasted_iota(jnp.int32, (ROWS, ROWS), 0), y, core)
                        c_id = lax.broadcasted_iota(jnp.int32, (ROWS, ROWS), 1)
                        c = jnp.where(c_id <= r_id, c, -BIG)
                    parts += [c[:, :DIM], c[:, DIM:]]
                top = parts[0]
                for c in parts[1:]:
                    top = jnp.maximum(top, c)
                top = jnp.broadcast_to(jnp.max(top, axis=1, keepdims=True), (ROWS, DIM))
                if not opening:
                    old = state_in[2][h]
                    top = jnp.maximum(old, top)
                    keep = jnp.exp2((old - top) * SCALE)
                p = [jnp.exp2((c - top) * SCALE).astype(BF16) for c in parts]
                mixed = jnp.dot(
                    jnp.concatenate(p, axis=1), va_ref[: m * ROWS, :], preferred_element_type=F32
                )
                acc, tot = mixed[:, :DIM], mixed[:, DIM:]
                if not opening:
                    acc = acc + state_in[0][h] * keep
                    tot = tot + state_in[1][h] * keep
            else:
                acc, tot, top = state_in[0][h], state_in[1][h], state_in[2][h]
            if final:
                res = (acc / tot).astype(BF16)
                for i, out in enumerate(outs):
                    out[:, cols] = res[i * 2 * SHARE : (i + 1) * 2 * SHARE, :]
            else:
                acc_out[h] = acc
                tot_out[h] = tot
                top_out[h] = top

    if opening:
        fold(n)
    else:
        for m in range(n + 1):
            pl.when(front == m)(functools.partial(fold, m))


def attend_part(lengths, q, parts, state=None, final=False):
    kinds = tuple(k for ks, _ in parts for k in ks)
    n = len(kinds)
    opening = state is None
    arrays = list(q)
    for _, a in parts:
        arrays += list(a) if isinstance(a, tuple) else [a]
    arrays += list(state or ())
    part = jax.ShapeDtypeStruct((HEADS, ROWS, DIM), F32)
    if final:
        outs = [jax.ShapeDtypeStruct((2 * SHARE, HEADS * DIM), BF16)] * NY
    else:
        outs = [part] * 3
        if opening:
            outs += [jax.ShapeDtypeStruct((ROWS, HEADS * DIM), BF16), jax.ShapeDtypeStruct((ROWS, DIM), BF16)]
    return pl.pallas_call(
        functools.partial(attend, kinds, opening, final),
        out_shape=outs,
        in_specs=[SMEM] + [VMEM] * len(arrays),
        out_specs=[VMEM] * len(outs),
        scratch_shapes=[pltpu.VMEM((2 * DIM, n * ROWS), BF16), pltpu.VMEM((n * ROWS, 2 * DIM), BF16)],
        cost_estimate=pl.CostEstimate(
            flops=8 * HEADS * ROWS * ROWS * DIM * n,
            bytes_accessed=1 << 20,
            transcendentals=HEADS * ROWS * ROWS * n,
        ),
        compiler_params=pltpu.CompilerParams(vmem_limit_bytes=16 * 2**20),
        name="attend",
    )(lengths, *arrays)


def lay_out(*refs):
    _, y, core = position()
    pieces, got, out, sems = refs[:NY], refs[NY], refs[NY + 1], refs[NY + 2]
    width = HEADS * DIM
    copies = []
    for d in range(NY):
        for k in range(2):
            src = got.at[d] if k else pieces[d].at[pl.ds(0, SHARE), :]
            at = pl.multiple_of((((y ^ d) << 1) + (core ^ k)) * width, width)
            copies.append(pltpu.make_async_copy(src, out.at[:, pl.ds(at, width)], sems.at[2 * d + k]))
    for c in copies:
        c.start()
    for c in copies:
        c.wait()


def exchange(pieces):
    size = lax.axis_size("kvh")
    flip = lambda m: [(i, i ^ m) for i in range(size)]
    held = {0: pieces[0]}
    for d in (2, 1, 3):
        held[d] = lax.ppermute(pieces[d], "kvh", flip(2 * d))
    held = [held[d] for d in range(NY)]
    got = lax.ppermute(jnp.stack([h[SHARE:] for h in held]), "kvh", flip(1))
    anywhere = pl.BlockSpec(memory_space=pl.ANY)
    return pl.pallas_call(
        lay_out,
        out_shape=jax.ShapeDtypeStruct((SHARE, size * HEADS * DIM), BF16),
        in_specs=[VMEM] * (NY + 1),
        out_specs=anywhere,
        scratch_shapes=[pltpu.SemaphoreType.DMA((2 * NY,))],
        compiler_params=pltpu.CompilerParams(vmem_limit_bytes=16 * 2**20),
        name="lay_out",
    )(*held, got)


def per_device(queries, keys, values, doc_lengths):
    size = lax.axis_size("ctx")
    down = [(i, (i + NX) % size) for i in range(size)]
    flip = lambda d: [(i, i ^ d) for i in range(size)]
    place = lax.axis_index("ctx")
    x = place % NX
    send = functools.partial(lax.ppermute, axis_name="ctx")
    own = jnp.stack([keys, values])
    one = jnp.stack([send(keys, perm=down), send(values, perm=down)])
    across = send(own, perm=flip(2))
    two = send(one, perm=down)
    p_one = ((("z", 1),), one)
    one, mine = lax.optimization_barrier((one, own))
    p_own = ((("z", 0),), mine)
    *state, qp, qa = attend_part(doc_lengths, (queries,), [p_own])
    two, state = lax.optimization_barrier((two, state))
    one_across = send(across, perm=down)
    low = jnp.stack([one, jnp.where(x & 1 == 0, own, two)])
    high = jnp.stack([one, jnp.where(x & 2 == 0, own, two)])
    near = send(low, perm=flip(1))
    far = send(high, perm=flip(3))
    two_across = send(one_across, perm=down)
    p_two = ((("z", 2),), two)
    p_across = ((("row", 2),), one_across)
    p_near = ((("row", 1), ("mix", 1)), near)
    p_far = ((("row", 3), ("mix", 3)), far)
    p_either = ((("either", 2),), (across, two_across))
    state = attend_part(doc_lengths, (qp, qa), [p_one, p_two, p_across], state)
    last = [p_near, p_far, p_either]
    pieces = attend_part(doc_lengths, (qp, qa), last, state, True)
    return exchange(pieces)


def solution(mesh):
    in_specs = (P("ctx", "kvh"), P("ctx", "kvh"), P("ctx", "kvh"), P())
    out_specs = P(("ctx", "kvh"), None)
    return jax.shard_map(
        per_device, mesh=mesh, in_specs=in_specs, out_specs=out_specs, check_vma=False
    )
```

```python
import functools
import math

import jax
import jax.numpy as jnp
from jax import lax
from jax.experimental import pallas as pl
from jax.experimental.pallas import tpu as pltpu
from jax.sharding import PartitionSpec as P

HEADS = 8
DIM = 128
ROWS = 256
NDOCS = 16
NX = 4
NY = 4
SHARE = 32
BIG = float(2**18)
SCALE = math.log2(math.e) / DIM**0.5
F32 = jnp.float32
BF16 = jnp.bfloat16
VMEM = pl.BlockSpec(memory_space=pltpu.VMEM)
SMEM = pl.BlockSpec(memory_space=pltpu.SMEM)


def bounds(len_ref):
    lane = lax.broadcasted_iota(jnp.int32, (1, DIM), 1)
    first = jnp.full((1, DIM), 2**30, jnp.int32)
    last = jnp.full((1, DIM), 2**30, jnp.int32)
    first = jnp.where(lane == NDOCS, -(2**30), first)
    last = jnp.where(lane == NDOCS, 0, last)
    at = jnp.int32(0)
    for d in range(NDOCS):
        first = jnp.where(lane == d, at, first)
        at = at + len_ref[d]
        last = jnp.where(lane == d, at, last)
    return first, last


def position():
    kvh = lax.axis_index("kvh").astype(jnp.int32)
    return lax.axis_index("ctx").astype(jnp.int32), kvh // 2, kvh % 2


def reach(len_ref, place):
    at = jnp.int32(0)
    begin = jnp.int32(0)
    for d in range(NDOCS):
        begin = jnp.where(at <= place * ROWS, at, begin)
        at = at + len_ref[d]
    return begin


def own_row(r, y, core):
    return ((r & ~63) ^ (y << 6)) | ((r & 32) ^ (core << 5)) | (r & 31)


def block_of(kind, d, place, x):
    row = place - x
    if kind == "z":
        return place - NX * d
    if kind == "row":
        return row - NX + (x ^ d)
    other = x ^ d
    return jnp.where(other < x, row, row - 2 * NX) + other


def attend(kinds, opening, final, *refs):
    n = len(kinds)
    len_ref = refs[0]
    rest = list(refs[1:])
    place, y, core = position()
    x = lax.rem(place, NX)
    q_ref = rest.pop(0)
    if not opening:
        qa_ref = rest.pop(0)
    kv = []
    while len(kv) < n:
        ref = rest.pop(0)
        if kinds[len(kv)] == ("either", 2):
            kv.append((ref, rest.pop(0)))
        elif len(ref.shape) == 4:
            kv += [ref.at[0], ref.at[1]]
        else:
            kv.append(ref)
    if not opening:
        state_in = rest[:3]
        rest = rest[3:]
    outs = rest[:-2]
    ka_ref, va_ref = rest[-2:]
    if not final:
        acc_out, tot_out, top_out = outs[:3]
        if opening:
            qp_ref, qa_ref = outs[3:]
    first, last = bounds(len_ref)
    if opening:
        for m in range(ROWS // SHARE):
            start = pl.multiple_of(own_row(m * SHARE, y, core), SHARE)
            qp_ref[m * SHARE : (m + 1) * SHARE, :] = q_ref[pl.ds(start, SHARE), :]
        pos = place * ROWS + own_row(lax.broadcasted_iota(jnp.int32, (ROWS, DIM), 0), y, core)
        qa_ref[...] = jnp.where((pos >= first) & (pos < last), 0.0, -BIG).astype(BF16)
        q_ref = qp_ref
    front = jnp.int32(0)
    begin = reach(len_ref, place)
    va_ref[:, DIM:] = jnp.ones((n * ROWS, DIM), BF16)
    for b, (kind, d) in enumerate(kinds):
        start = block_of(kind, d, place, x) * ROWS

        def place_block(at, b=b, kind=kind, d=d, start=start):
            if kind == "either":
                late = x < (x ^ d)
                key = jnp.where(late, kv[b][1][0], kv[b][0][0])
                val = jnp.where(late, kv[b][1][1], kv[b][0][1])
            else:
                key, val = kv[b][0], kv[b][1]
            pos = start + lax.broadcasted_iota(jnp.int32, (ROWS, DIM), 0)
            ka_ref[:DIM, at] = key.T
            ka_ref[DIM:, at] = jnp.where((pos >= first) & (pos < last), 1.0, 0.0).astype(BF16).T
            va_ref[at, :DIM] = val

        if opening:
            place_block(slice(b * ROWS, (b + 1) * ROWS))
        else:
            used = start + ROWS > begin
            at = pl.ds(pl.multiple_of(front * ROWS, ROWS), ROWS)
            pl.when(used)(functools.partial(place_block, at))
            front = front + used.astype(jnp.int32)

    def scores(h, m):
        qq = jnp.concatenate([q_ref[:, h * DIM : (h + 1) * DIM], qa_ref[...]], axis=1)
        return jnp.dot(qq, ka_ref[:, : m * ROWS], preferred_element_type=F32)

    def fold(m):
        ahead = scores(0, m) if m else None
        for h in range(HEADS):
            cols = slice(h * DIM, (h + 1) * DIM)
            if m:
                s = ahead
                if h + 1 < HEADS:
                    ahead = scores(h + 1, m)
                parts = []
                for b in range(m):
                    c = s[:, b * ROWS : (b + 1) * ROWS]
                    if kinds[b] == ("z", 0):
                        r_id = own_row(lax.broadcasted_iota(jnp.int32, (ROWS, ROWS), 0), y, core)
                        c_id = lax.broadcasted_iota(jnp.int32, (ROWS, ROWS), 1)
                        c = jnp.where(c_id <= r_id, c, -BIG)
                    parts += [c[:, :DIM], c[:, DIM:]]
                top = parts[0]
                for c in parts[1:]:
                    top = jnp.maximum(top, c)
                top = jnp.broadcast_to(jnp.max(top, axis=1, keepdims=True), (ROWS, DIM))
                if not opening:
                    old = state_in[2][h]
                    top = jnp.maximum(old, top)
                    keep = jnp.exp2((old - top) * SCALE)
                p = [jnp.exp2((c - top) * SCALE).astype(BF16) for c in parts]
                mixed = jnp.dot(
                    jnp.concatenate(p, axis=1), va_ref[: m * ROWS, :], preferred_element_type=F32
                )
                acc, tot = mixed[:, :DIM], mixed[:, DIM:]
                if not opening:
                    acc = acc + state_in[0][h] * keep
                    tot = tot + state_in[1][h] * keep
            else:
                acc, tot, top = state_in[0][h], state_in[1][h], state_in[2][h]
            if final:
                res = (acc / tot).astype(BF16)
                for i, out in enumerate(outs):
                    out[:, cols] = res[i * 2 * SHARE : (i + 1) * 2 * SHARE, :]
            else:
                acc_out[h] = acc
                tot_out[h] = tot
                top_out[h] = top

    if opening:
        fold(n)
    else:
        for m in range(n + 1):
            pl.when(front == m)(functools.partial(fold, m))


def attend_part(lengths, q, parts, state=None, final=False):
    kinds = tuple(k for ks, _ in parts for k in ks)
    n = len(kinds)
    opening = state is None
    arrays = list(q)
    for _, a in parts:
        arrays += list(a) if isinstance(a, tuple) else [a]
    arrays += list(state or ())
    part = jax.ShapeDtypeStruct((HEADS, ROWS, DIM), F32)
    if final:
        outs = [jax.ShapeDtypeStruct((2 * SHARE, HEADS * DIM), BF16)] * NY
    else:
        outs = [part] * 3
        if opening:
            outs += [jax.ShapeDtypeStruct((ROWS, HEADS * DIM), BF16), jax.ShapeDtypeStruct((ROWS, DIM), BF16)]
    return pl.pallas_call(
        functools.partial(attend, kinds, opening, final),
        out_shape=outs,
        in_specs=[SMEM] + [VMEM] * len(arrays),
        out_specs=[VMEM] * len(outs),
        scratch_shapes=[pltpu.VMEM((2 * DIM, n * ROWS), BF16), pltpu.VMEM((n * ROWS, 2 * DIM), BF16)],
        cost_estimate=pl.CostEstimate(
            flops=8 * HEADS * ROWS * ROWS * DIM * n,
            bytes_accessed=1 << 20,
            transcendentals=HEADS * ROWS * ROWS * n,
        ),
        compiler_params=pltpu.CompilerParams(vmem_limit_bytes=16 * 2**20),
        name="attend",
    )(lengths, *arrays)


def lay_out(*refs):
    _, y, core = position()
    pieces, got, out, sems = refs[:NY], refs[NY], refs[NY + 1], refs[NY + 2]
    width = HEADS * DIM
    copies = []
    for d in range(NY):
        for k in range(2):
            src = got.at[d] if k else pieces[d].at[pl.ds(0, SHARE), :]
            at = pl.multiple_of((((y ^ d) << 1) + (core ^ k)) * width, width)
            copies.append(pltpu.make_async_copy(src, out.at[:, pl.ds(at, width)], sems.at[2 * d + k]))
    for c in copies:
        c.start()
    for c in copies:
        c.wait()


def exchange(pieces):
    size = lax.axis_size("kvh")
    flip = lambda m: [(i, i ^ m) for i in range(size)]
    held = {0: pieces[0]}
    for d in (2, 1, 3):
        held[d] = lax.ppermute(pieces[d], "kvh", flip(2 * d))
    held = [held[d] for d in range(NY)]
    got = lax.ppermute(jnp.stack([h[SHARE:] for h in held]), "kvh", flip(1))
    anywhere = pl.BlockSpec(memory_space=pl.ANY)
    return pl.pallas_call(
        lay_out,
        out_shape=jax.ShapeDtypeStruct((SHARE, size * HEADS * DIM), BF16),
        in_specs=[VMEM] * (NY + 1),
        out_specs=anywhere,
        scratch_shapes=[pltpu.SemaphoreType.DMA((2 * NY,))],
        compiler_params=pltpu.CompilerParams(vmem_limit_bytes=16 * 2**20),
        name="lay_out",
    )(*held, got)


def per_device(queries, keys, values, doc_lengths):
    size = lax.axis_size("ctx")
    down = [(i, (i + NX) % size) for i in range(size)]
    flip = lambda d: [(i, i ^ d) for i in range(size)]
    place = lax.axis_index("ctx")
    x = place % NX
    send = functools.partial(lax.ppermute, axis_name="ctx")
    own = jnp.stack([keys, values])
    one = jnp.stack([send(keys, perm=down), send(values, perm=down)])
    across = send(own, perm=flip(2))
    two = send(one, perm=down)
    p_one = ((("z", 1),), one)
    one_across = send(one, perm=flip(2))
    one, mine, across = lax.optimization_barrier((one, own, across))
    p_own = ((("z", 0),), mine)
    *state, qp, qa = attend_part(doc_lengths, (queries,), [p_own])
    two, state = lax.optimization_barrier((two, state))
    low = jnp.stack([one, jnp.where(x & 1 == 0, own, two)])
    high = jnp.stack([one, jnp.where(x & 2 == 0, own, two)])
    near = send(low, perm=flip(1))
    far = send(high, perm=flip(3))
    two_across = send(one_across, perm=down)
    p_two = ((("z", 2),), two)
    p_across = ((("row", 2),), one_across)
    p_near = ((("row", 1), ("mix", 1)), near)
    p_far = ((("row", 3), ("mix", 3)), far)
    p_either = ((("either", 2),), (across, two_across))
    state = attend_part(doc_lengths, (qp, qa), [p_one, p_two, p_across], state)
    last = [p_near, p_far, p_either]
    pieces = attend_part(doc_lengths, (qp, qa), last, state, True)
    return exchange(pieces)


def solution(mesh):
    in_specs = (P("ctx", "kvh"), P("ctx", "kvh"), P("ctx", "kvh"), P())
    out_specs = P(("ctx", "kvh"), None)
    return jax.shard_map(
        per_device, mesh=mesh, in_specs=in_specs, out_specs=out_specs, check_vma=False
    )
```
